768 devices in a mesh: inter: 96 (over y, z_lo, x), intra: 8 (over z_hi, core).
Axes of the slice: x: 4, y: 8, z: 12 (z_hi: 4, z_lo: 3; z = z_hi * 3 + z_lo), core: 2. Of those that a mesh axis runs over, the one named last changes fastest.
Arguments:
- activations: bfloat16 [8, 192, 1, 5120], P('intra'), may hold values from -6 to 6
- hidden_cot: bfloat16 [8, 192, 1, 6912], P('intra', None, None, 'inter'), may hold values from -6 to 6
- weight: float32 [276480, 256], P(('inter', 'intra')), may hold values from -0.078125 to 0.078125
Outputs:
- weight_grad: float32 [276480, 256], P(('inter', 'intra'))
- input_grad: bfloat16 [8, 192, 1, 5120], P('intra', 'inter')
The draws below stay inside these ranges and needn't reach their ends.
All inputs are finite; a program needn't handle non-finite values. Where the reference program divides by a largest or mean magnitude, that divisor is 1e-20 or more.
Results may differ from the reference program's by a relative error of at most 0.024.
Values may be sent and summed in bfloat16 or wider, within the bound.
No kernel may reach another device: no remote copies, remote signals or barrier semaphores. Data moves between devices by JAX's collectives and lax.ppermute only.
A program may use at most 32 MiB of HBM per device.

```python
import math
import jax
import jax.numpy as jnp
from jax import lax

D = 5120
HID = 6912
QB = 256
MB = 1
TOK_MB = 192
SLOTS = 8
HID_G = 72
BLOCKS = 276480
N_INTER = 96


def level_of(rng, extent, pieces, smallest, top_value):
    factor_of, own = 1.0, jax.random.fold_in(rng, 6)
    for position, blocks in pieces:
        heights = jnp.exp(jax.random.uniform(jax.random.fold_in(own, position), (blocks,), jnp.float32, smallest / len(pieces), top_value / len(pieces)))
        factor_of = factor_of * jnp.repeat(heights, extent[position] // blocks).reshape([-1 if axis == position else 1 for axis in range(len(extent))])
    return factor_of


def centred(stream_key, shape, width, most, pieces=(), held_as=jnp.bfloat16):
    drawn = jax.random.normal(stream_key, shape, jnp.float32) * width
    if len(pieces) > 0:
        drawn = level_of(stream_key, shape, pieces, -0.22, 0.18) * drawn
    return jnp.clip(drawn, min=-most, max=most).astype(held_as)


def setup_inputs(seed: int = 0) -> dict:
    arg_keys = jax.random.split(jax.random.key(seed), 4)
    activations = centred(arg_keys[0], (SLOTS, TOK_MB, MB, D), 1.0, 6.0, ((0, 8),))
    hidden_cot = centred(arg_keys[1], (SLOTS, TOK_MB, MB, HID), 1.0, 6.0, ((0, 8), (3, 96)))
    weight = centred(arg_keys[2], (BLOCKS, QB), D ** -0.5, 0.078125, ((0, 768),), jnp.float32)
    return dict(activations=activations, hidden_cot=hidden_cot, weight=weight)


EPS = 1e-06

def quantize(blocks):
    scales = (lax.optimization_barrier(jnp.max(jnp.abs(blocks), axis=-1)) + EPS).astype(jnp.bfloat16)
    values = (blocks / scales.astype(jnp.float32)[..., None]).astype(jnp.bfloat16)
    return (lax.optimization_barrier(values), scales)

def dequantize(values, scales):
    return values.astype(jnp.float32) * scales.astype(jnp.float32)[..., None]

def reference(activations, hidden_cot, weight):
    values, scales = quantize(weight)
    w_all = dequantize(values, scales).astype(jnp.bfloat16).reshape(N_INTER, 2, HID_G, D)
    gate_w = w_all[:, 0].reshape(HID, D)
    up_w = w_all[:, 1].reshape(HID, D)
    rows = activations.reshape(SLOTS * TOK_MB * MB, D)
    cotangent = hidden_cot.reshape(SLOTS * TOK_MB * MB, HID).astype(jnp.float32)
    gate = jnp.dot(rows, gate_w.T, preferred_element_type=jnp.float32)
    upper = jnp.dot(rows, up_w.T, preferred_element_type=jnp.float32)
    sigmoid_gate = jax.nn.sigmoid(gate)
    grad_gate = (cotangent * upper * sigmoid_gate * (1.0 + gate * (1.0 - sigmoid_gate))).astype(jnp.bfloat16)
    grad_up = (cotangent * gate * sigmoid_gate).astype(jnp.bfloat16)
    summed_in = jnp.dot(grad_gate, gate_w, preferred_element_type=jnp.float32) + jnp.dot(grad_up, up_w, preferred_element_type=jnp.float32)
    input_grad = summed_in.astype(jnp.bfloat16).reshape(SLOTS, TOK_MB, MB, D)
    block_rows = TOK_MB * MB

    def slot_step(total, index):
        start = (index * block_rows).astype(jnp.int32)
        tokens = lax.dynamic_slice_in_dim(rows, start, block_rows, 0)
        part_gate = lax.dynamic_slice_in_dim(grad_gate, start, block_rows, 0)
        part_up = lax.dynamic_slice_in_dim(grad_up, start, block_rows, 0)
        local_gate = jnp.dot(part_gate.T, tokens, preferred_element_type=jnp.float32).reshape(N_INTER, HID_G, D)
        local_up = jnp.dot(part_up.T, tokens, preferred_element_type=jnp.float32).reshape(N_INTER, HID_G, D)
        local_grad = jnp.stack([local_gate, local_up], axis=1).reshape(BLOCKS, QB)
        g_values, g_scales = quantize(local_grad)
        return (total + dequantize(g_values, g_scales), None)
    total, unused = lax.scan(slot_step, jnp.zeros((BLOCKS, QB), jnp.float32), jnp.arange(SLOTS, dtype=jnp.int32))
    weight_grad = total * (1.0 / math.sqrt(MB * TOK_MB * SLOTS))
    return (weight_grad, input_grad)
```

```python
import functools
import math

import jax
import jax.numpy as jnp
from jax import lax
from jax.experimental import pallas as pl
from jax.experimental.pallas import tpu as pltpu
from jax.sharding import Mesh, PartitionSpec as P

EPS = 1e-06
LANES = 128
F32 = jnp.float32
BF16 = jnp.bfloat16
VMEM = pl.BlockSpec(memory_space=pltpu.VMEM)
PARAMS = pltpu.CompilerParams(vmem_limit_bytes=40 << 20)


def requantized(blocks):
    scales = (jnp.max(jnp.abs(blocks), axis=-1, keepdims=True) + EPS).astype(BF16).astype(F32)
    values = (blocks / scales).astype(BF16).astype(F32)
    return values * scales


def quantize_kernel(w_ref, out_ref):
    out_ref[...] = requantized(w_ref[...]).astype(BF16)


def quantize_weight(weight):
    return pl.pallas_call(
        quantize_kernel,
        out_shape=jax.ShapeDtypeStruct(weight.shape, BF16),
        in_specs=[VMEM],
        out_specs=VMEM,
    )(weight)


def permutation(tokens, nx, ny, nz):
    own = tokens // (nx * ny * nz)
    new = lax.broadcasted_iota(jnp.int32, (tokens, tokens), 0)
    old = lax.broadcasted_iota(jnp.int32, (tokens, tokens), 1)
    r = new % own
    y = (new // own) % ny
    z = (new // (own * ny)) % nz
    x = new // (own * ny * nz)
    source = ((y * nz + z) * nx + x) * own + r
    return (source == old).astype(BF16)


def gate_kernel(plan, sizes, pos_ref, *refs):
    pieces, refs = refs[: len(plan)], refs[len(plan) :]
    x_ref, c_ref, perm_ref, part_ref, keep_ref, send_ref, w32, wmat = refs
    zh, core = pos_ref[0], pos_ref[1]
    n_z, chunk = sizes
    rows = wmat.shape[0]
    block = pieces[0].shape[1]
    per_row = w32.shape[1] // rows
    lanes = w32.shape[2]
    halves = block // lanes
    for (dz, dc, first), piece in zip(plan, pieces):
        at = (dc * n_z + lax.rem(zh + dz, n_z)) * chunk + first
        at = pl.multiple_of(at, 8)
        for k in range(halves):
            w32[k, pl.ds(at, piece.shape[0]), :] = piece[:, k * lanes : (k + 1) * lanes].astype(F32)
    proj = jnp.zeros((rows, x_ref.shape[0]), F32)
    for b in range(per_row):
        columns = slice(b * block, (b + 1) * block)
        w = jnp.concatenate(
            [w32[k, pl.ds(b, rows, stride=per_row), :] for k in range(halves)], axis=1
        ).astype(BF16)
        wmat[:, columns] = w
        proj += lax.dot_general(
            w, x_ref[:, columns], (((1,), (1,)), ((), ())), preferred_element_type=F32
        )
    quarter = rows // 4
    eighth = quarter // 2
    cot = c_ref[...].astype(F32).T
    low = jnp.concatenate([cot[:eighth], cot[quarter : quarter + eighth]], axis=0)
    high = jnp.concatenate([cot[eighth:quarter], cot[quarter + eighth :]], axis=0)
    pre = []
    for dc in range(2):
        base = dc * 2 * quarter
        gate = proj[base : base + quarter]
        upper = proj[base + quarter : base + 2 * quarter]
        c = jnp.where(core == dc, low, high)
        sig = jax.nn.sigmoid(gate)
        pre.append(c * upper * sig * (1.0 + gate * (1.0 - sig)))
        pre.append(c * gate * sig)
    keep = jnp.concatenate(pre[:2], axis=0)
    send = jnp.concatenate(pre[2:], axis=0)
    keep_ref[...] = keep.astype(BF16)
    send_ref[...] = send.astype(BF16)
    pre = jnp.concatenate([keep, send], axis=0).astype(BF16)
    pre = lax.dot_general(
        perm_ref[...], pre, (((1,), (1,)), ((), ())), preferred_element_type=F32
    ).astype(BF16)
    for b in range(per_row):
        columns = slice(b * block, (b + 1) * block)
        part_ref[:, columns] = jnp.dot(
            pre, wmat[:, columns], preferred_element_type=F32
        ).astype(BF16)


def gate_part(pos, plan, pieces, n_z, chunk, x, cot, perm):
    tokens, width = x.shape
    rows = 2 * cot.shape[1]
    block = pieces[0].shape[1]
    return pl.pallas_call(
        functools.partial(gate_kernel, plan, (n_z, chunk)),
        out_shape=(
            jax.ShapeDtypeStruct((tokens, width), BF16),
            jax.ShapeDtypeStruct((rows // 2, tokens), BF16),
            jax.ShapeDtypeStruct((rows // 2, tokens), BF16),
        ),
        in_specs=[pl.BlockSpec(memory_space=pltpu.SMEM)] + [VMEM] * (len(pieces) + 3),
        out_specs=(VMEM,) * 3,
        scratch_shapes=[
            pltpu.VMEM((block // LANES, 2 * n_z * chunk, LANES), F32),
            pltpu.VMEM((rows, width), BF16),
        ],
        compiler_params=PARAMS,
    )(pos, *pieces, x, cot, perm)


def weight_grad_kernel(n_z, pos_ref, mine_ref, got_ref, x_ref, xo_ref, own, nxt, prv, far_a, far_b, g32):
    zh = pos_ref[0]
    rows = mine_ref.shape[0]
    chunk, block = own.shape
    per_row = n_z * chunk // rows
    lanes = g32.shape[2]
    for b in range(per_row):
        columns = slice(b * block, (b + 1) * block)
        local = requantized(
            jnp.dot(mine_ref[...], x_ref[:, columns], preferred_element_type=F32)
        ) + requantized(jnp.dot(got_ref[...], xo_ref[:, columns], preferred_element_type=F32))
        for k in range(block // lanes):
            g32[k, pl.ds(b, rows, stride=per_row), :] = local[:, k * lanes : (k + 1) * lanes]
    half = far_a.shape[0]
    for out, dz, first in ((own, 0, 0), (nxt, 1, 0), (prv, n_z - 1, 0), (far_a, 2, 0), (far_b, 2, half)):
        at = pl.multiple_of(lax.rem(zh + dz, n_z) * chunk + first, 8)
        for k in range(block // lanes):
            out[:, k * lanes : (k + 1) * lanes] = g32[k, pl.ds(at, out.shape[0]), :].astype(out.dtype)


def weight_grad_part(pos, mine, got, x, x_other, n_z, chunk, half, block):
    shape = jax.ShapeDtypeStruct
    return pl.pallas_call(
        functools.partial(weight_grad_kernel, n_z),
        out_shape=(
            shape((chunk, block), F32),
            shape((chunk, block), F32),
            shape((chunk, block), F32),
            shape((half, block), BF16),
            shape((chunk - half, block), BF16),
        ),
        in_specs=[pl.BlockSpec(memory_space=pltpu.SMEM)] + [VMEM] * 4,
        out_specs=(VMEM,) * 5,
        scratch_shapes=[pltpu.VMEM((block // LANES, n_z * chunk, LANES), F32)],
        compiler_params=PARAMS,
    )(pos, mine, got, x, x_other)


def relay_kernel(nxt, prv, far_a, far_b, out_nxt, out_prv):
    half = far_a.shape[0]
    out_nxt[:half] = (nxt[:half] + far_a[...].astype(F32)).astype(BF16)
    out_nxt[half:] = nxt[half:].astype(BF16)
    out_prv[:half] = prv[:half].astype(BF16)
    out_prv[half:] = (prv[half:] + far_b[...].astype(F32)).astype(BF16)


def relay(nxt, prv, far_a, far_b):
    return pl.pallas_call(
        relay_kernel,
        out_shape=(jax.ShapeDtypeStruct(nxt.shape, BF16),) * 2,
        in_specs=[VMEM] * 4,
        out_specs=(VMEM,) * 2,
    )(nxt, prv, far_a, far_b)


def step(array, axis, by):
    n = lax.axis_size(axis)
    return lax.ppermute(array, axis, [(i, (i + by) % n) for i in range(n)])


def summed_pieces(array, axis):
    got = lax.all_to_all(array, axis, split_axis=0, concat_axis=0, tiled=True)
    return jnp.sum(got.astype(F32), axis=0).astype(BF16)


def body(activations, hidden_cot, weight):
    tok = activations.shape[1] * activations.shape[2]
    width = activations.shape[3]
    hidden = hidden_cot.shape[3]
    chunk, block = weight.shape
    half = (chunk // 2 + 15) // 16 * 16
    n_x, n_y, n_l, n_z = (lax.axis_size(a) for a in ("x", "y", "zl", "zh"))
    x = activations.reshape(tok, width)
    cot = hidden_cot.reshape(tok, hidden)
    pos = jnp.stack([lax.axis_index("zh"), lax.axis_index("c")]).astype(jnp.int32)
    perm = permutation(tok, n_x, n_y, n_l)

    own = quantize_weight(weight)
    before = step(own, "zh", 1)
    after = step(own, "zh", -1)
    x_other = step(x, "c", 1)
    own_o = step(own, "c", 1)
    far_a = step(before[:half], "zh", 1)
    far_b = step(after[half:], "zh", -1)
    before_o = step(before, "c", 1)
    after_o = step(after, "c", 1)
    far_ao = step(far_a, "c", 1)
    far_bo = step(far_b, "c", 1)
    last = n_z - 1
    plan = ((0, 0, 0), (last, 0, 0), (1, 0, 0), (2, 0, 0), (2, 0, half))
    plan = plan + tuple((dz, 1, first) for dz, _, first in plan)
    pieces = (own, before, after, far_a, far_b, own_o, before_o, after_o, far_ao, far_bo)
    part, keep, send = gate_part(pos, plan, pieces, n_z, chunk, x, cot, perm)

    rows = summed_pieces(part.reshape(n_x, tok // n_x, width), "x")
    rows = summed_pieces(rows.reshape(n_l, -1, width), "zl")
    rows = summed_pieces(rows.reshape(n_y, -1, width), "y")
    input_grad = rows.reshape(1, -1, activations.shape[2], width)

    got = step(send, "c", 1)
    g_own, g_nxt, g_prv, g_fa, g_fb = weight_grad_part(
        pos, keep, got, x, x_other, n_z, chunk, half, block
    )
    r_a = step(g_fa, "zh", 1)
    r_b = step(g_fb, "zh", -1)
    s_nxt, s_prv = relay(g_nxt, g_prv, r_a, r_b)
    from_prv = step(s_nxt, "zh", 1)
    from_nxt = step(s_prv, "zh", -1)
    total = g_own + from_prv.astype(F32) + from_nxt.astype(F32)
    weight_grad = total * (1.0 / math.sqrt(tok * n_z * lax.axis_size("c")))
    return (weight_grad, input_grad)


def solution(mesh):
    fine = Mesh(mesh.devices.reshape(8, 3, 4, 4, 2), ("y", "zl", "x", "zh", "c"))
    inter, intra = ("y", "zl", "x"), ("zh", "c")
    return jax.shard_map(
        body,
        mesh=fine,
        in_specs=(
            P(intra, None, None, None),
            P(intra, None, None, inter),
            P(inter + intra, None),
        ),
        out_specs=(P(inter + intra, None), P(intra, inter, None, None)),
        check_vma=False,
    )
```

```python
import functools
import math

import jax
import jax.numpy as jnp
from jax import lax
from jax.experimental import pallas as pl
from jax.experimental.pallas import tpu as pltpu
from jax.sharding import Mesh, PartitionSpec as P

EPS = 1e-06
LANES = 128
INTER = ("yh", "yl", "zl", "x")
FIRST = ("x", "yl")
SECOND = ("yh", "zl")
F32 = jnp.float32
BF16 = jnp.bfloat16
VMEM = pl.BlockSpec(memory_space=pltpu.VMEM)
HBM = pl.BlockSpec(memory_space=pltpu.HBM)
SPANS = 5
PARAMS = pltpu.CompilerParams(vmem_limit_bytes=40 << 20)


def requantized(blocks):
    scales = (jnp.max(jnp.abs(blocks), axis=-1, keepdims=True) + EPS).astype(BF16).astype(F32)
    values = (blocks / scales).astype(BF16).astype(F32)
    return values * scales


def quantize_kernel(w_ref, out_ref):
    out_ref[...] = requantized(w_ref[...]).astype(BF16)


def quantize_weight(weight):
    return pl.pallas_call(
        quantize_kernel,
        out_shape=jax.ShapeDtypeStruct(weight.shape, BF16),
        in_specs=[VMEM],
        out_specs=VMEM,
    )(weight)


def quotient(number, by, count):
    return sum((number >= by * k).astype(jnp.int32) for k in range(1, count))


def permutation(tokens, held, wanted):
    new = lax.broadcasted_iota(jnp.int32, (tokens, tokens), 0)
    old = lax.broadcasted_iota(jnp.int32, (tokens, tokens), 1)
    sizes = dict(held)
    own = tokens // math.prod(sizes.values())
    index, rest, stride = {}, new, tokens
    for axis in wanted:
        stride //= sizes[axis]
        index[axis] = quotient(rest, stride, sizes[axis])
        rest = rest - index[axis] * stride
    source = jnp.zeros_like(new)
    for axis, size in held:
        source = source * size + index[axis]
    source = source * own + rest
    return (source == old).astype(F32).astype(BF16)


def gate_kernel(orders, pos_ref, wa_ref, wb_ref, x_hbm, c_ref, part_hbm, keep_ref, send_ref, *scratch):
    w32, wmat, x_ref, part_ref, sem_in, sem_out = scratch
    core = pos_ref[1]
    span = x_ref.shape[1] // SPANS
    spans = [slice(i * span, (i + 1) * span) for i in range(SPANS)]
    loads = [
        pltpu.make_async_copy(x_hbm.at[:, at], x_ref.at[:, at], sem_in.at[i])
        for i, at in enumerate(spans)
    ]
    stores = [
        pltpu.make_async_copy(part_ref.at[:, at], part_hbm.at[:, at], sem_out.at[i])
        for i, at in enumerate(spans)
    ]
    for load in loads:
        load.start()
    rows = wmat.shape[0]
    chunk, block = wa_ref.shape
    per_row = w32.shape[1] // rows
    lanes = w32.shape[2]
    halves = block // lanes
    for i, w_ref in enumerate((wa_ref, wb_ref)):
        for k in range(halves):
            half = w_ref[:, k * lanes : (k + 1) * lanes].astype(F32)
            w32[k, i * chunk : (i + 1) * chunk] = half
    proj = jnp.zeros((rows, x_ref.shape[0]), F32)
    for b in range(per_row):
        columns = slice(b * block, (b + 1) * block)
        if b * block % span == 0:
            loads[b * block // span].wait()
        w = jnp.concatenate(
            [w32[k, pl.ds(b, rows, stride=per_row), :] for k in range(halves)], axis=1
        ).astype(BF16)
        wmat[:, columns] = w
        proj += lax.dot_general(
            w, x_ref[:, columns], (((1,), (1,)), ((), ())), preferred_element_type=F32
        )
    quarter = rows // 4
    eighth = quarter // 2
    cot = c_ref[...].astype(F32)
    low = jnp.concatenate([cot[:eighth], cot[quarter : quarter + eighth]], axis=0)
    high = jnp.concatenate([cot[eighth:quarter], cot[quarter + eighth :]], axis=0)
    pre = []
    for dc in range(2):
        base = dc * 2 * quarter
        gate = proj[base : base + quarter]
        upper = proj[base + quarter : base + 2 * quarter]
        c = jnp.where(core == dc, low, high)
        sig = jax.nn.sigmoid(gate)
        pre.append(c * upper * sig * (1.0 + gate * (1.0 - sig)))
        pre.append(c * gate * sig)
    keep = jnp.concatenate(pre[:2], axis=0)
    send = jnp.concatenate(pre[2:], axis=0)
    keep_ref[...] = keep.astype(BF16)
    send_ref[...] = send.astype(BF16)
    pre = jnp.concatenate([keep, send], axis=0).astype(BF16)
    pre = lax.dot_general(
        permutation(x_ref.shape[0], *orders),
        pre,
        (((1,), (1,)), ((), ())),
        preferred_element_type=F32,
    ).astype(BF16)
    for b in range(per_row):
        columns = slice(b * block, (b + 1) * block)
        part_ref[:, columns] = jnp.dot(
            pre, wmat[:, columns], preferred_element_type=F32
        ).astype(BF16)
        if (b + 1) * block % span == 0:
            stores[b * block // span].start()
    for store in stores:
        store.wait()


def gate_part(orders, pos, w_mine, w_other, x, cot):
    tokens, width = x.shape
    rows = 2 * cot.shape[0]
    block = w_mine.shape[1]
    return pl.pallas_call(
        functools.partial(gate_kernel, orders),
        out_shape=(
            jax.ShapeDtypeStruct((tokens, width), BF16),
            jax.ShapeDtypeStruct((rows // 2, tokens), BF16),
            jax.ShapeDtypeStruct((rows // 2, tokens), BF16),
        ),
        in_specs=[pl.BlockSpec(memory_space=pltpu.SMEM), VMEM, VMEM, HBM, VMEM],
        out_specs=(HBM, VMEM, VMEM),
        scratch_shapes=[
            pltpu.VMEM((block // LANES, 2 * w_mine.shape[0], LANES), F32),
            pltpu.VMEM((rows, width), BF16),
            pltpu.VMEM((tokens, width), BF16),
            pltpu.VMEM((tokens, width), BF16),
            pltpu.SemaphoreType.DMA((SPANS,)),
            pltpu.SemaphoreType.DMA((SPANS,)),
        ],
        compiler_params=pltpu.CompilerParams(vmem_limit_bytes=61_600_000),
    )(pos, w_mine, w_other, x, cot)


def weight_grad_kernel(steps, pos_ref, mine_ref, got_ref, x_ref, xo_ref, *refs):
    outs, g32 = refs[: len(steps)], refs[len(steps)]
    zh = pos_ref[0]
    rows = mine_ref.shape[0]
    chunk, block = outs[0].shape
    n_z = len(steps)
    per_row = n_z * chunk // rows
    lanes = g32.shape[2]
    for b in range(per_row):
        columns = slice(b * block, (b + 1) * block)
        local = requantized(
            jnp.dot(mine_ref[...], x_ref[:, columns], preferred_element_type=F32)
        ) + requantized(jnp.dot(got_ref[...], xo_ref[:, columns], preferred_element_type=F32))
        for k in range(block // lanes):
            g32[k, pl.ds(b, rows, stride=per_row), :] = local[:, k * lanes : (k + 1) * lanes]
    for out, dz in zip(outs, steps):
        at = pl.multiple_of(lax.rem(zh + dz, n_z) * chunk, 8)
        for k in range(block // lanes):
            piece = g32[k, pl.ds(at, chunk), :]
            out[:, k * lanes : (k + 1) * lanes] = piece.astype(out.dtype)


def weight_grad_part(steps, pos, mine, got, x, x_other, chunk, block):
    return pl.pallas_call(
        functools.partial(weight_grad_kernel, steps),
        out_shape=[
            jax.ShapeDtypeStruct((chunk, block), BF16 if dz else F32) for dz in steps
        ],
        in_specs=[pl.BlockSpec(memory_space=pltpu.SMEM)] + [VMEM] * 4,
        out_specs=[VMEM] * len(steps),
        scratch_shapes=[pltpu.VMEM((block // LANES, len(steps) * chunk, LANES), F32)],
        compiler_params=PARAMS,
    )(pos, mine, got, x, x_other)


def total_kernel(scale, total_ref, *refs):
    total = total_ref[...]
    for piece in refs[:-1]:
        total = total + piece[...].astype(F32)
    refs[-1][...] = total * scale


def scaled_total(scale, total, pieces):
    return pl.pallas_call(
        functools.partial(total_kernel, scale),
        out_shape=jax.ShapeDtypeStruct(total.shape, F32),
        in_specs=[VMEM] * (1 + len(pieces)),
        out_specs=VMEM,
        cost_estimate=pl.CostEstimate(flops=10**11, bytes_accessed=0, transcendentals=0),
        compiler_params=PARAMS,
    )(total, *pieces)


def step(array, axis, by):
    n = lax.axis_size(axis)
    return lax.ppermute(array, axis, [(i, (i + by) % n) for i in range(n)])


def swapped(array):
    return lax.ppermute(array, "c", [(0, 1), (1, 0)])


def summed_pieces(pieces):
    return jnp.sum(pieces.astype(F32), axis=0).astype(BF16)


def spread(array, axes):
    return lax.all_to_all(array, axes, split_axis=0, concat_axis=0, tiled=True)


def body(activations, hidden_cot, weight):
    tok = activations.shape[1] * activations.shape[2]
    width = activations.shape[3]
    hidden = hidden_cot.shape[3]
    n_z = lax.axis_size("zh")
    x = activations.reshape(tok, width)
    cot = hidden_cot.reshape(tok, hidden).T
    pos = jnp.stack([lax.axis_index("zh"), lax.axis_index("c")]).astype(jnp.int32)
    chunk, block = weight.shape

    own = quantize_weight(weight)
    w_mine = lax.all_gather(own, "zh", axis=0, tiled=True)
    w_mine, x_late = lax.optimization_barrier((w_mine, x))
    w_other = swapped(w_mine)
    x_other = swapped(x_late)
    held = tuple((axis, lax.axis_size(axis)) for axis in INTER)
    part, keep, send = gate_part((held, FIRST + SECOND), pos, w_mine, w_other, x, cot)

    first = math.prod(lax.axis_size(axis) for axis in FIRST)
    second = math.prod(lax.axis_size(axis) for axis in SECOND)
    rows = spread(part.reshape(first, -1, width), FIRST)
    got = swapped(send)
    steps = (0, n_z // 2) + tuple(dz for dz in range(1, n_z) if dz != n_z // 2)
    total, *chunks = weight_grad_part(steps, pos, keep, got, x, x_other, chunk, block)
    rows, _ = lax.optimization_barrier((rows, chunks))
    arrived = [step(piece, "zh", dz) for piece, dz in zip(chunks, steps[1:])]
    rows = summed_pieces(rows)
    rows = spread(rows.reshape(second, -1, width), SECOND)
    input_grad = summed_pieces(rows).reshape(1, -1, activations.shape[2], width)
    scale = 1.0 / math.sqrt(tok * n_z * lax.axis_size("c"))
    weight_grad = scaled_total(scale, total, arrived)
    return (weight_grad, input_grad)


def solution(mesh):
    fine = Mesh(mesh.devices.reshape(4, 2, 3, 4, 4, 2), INTER + ("zh", "c"))
    return jax.shard_map(
        body,
        mesh=fine,
        in_specs=(
            P(("zh", "c"), None, None, None),
            P(("zh", "c"), None, None, INTER),
            P(INTER + ("zh", "c"), None),
        ),
        out_specs=(P(INTER + ("zh", "c"), None), P(("zh", "c"), INTER, None, None)),
        check_vma=False,
    )
```

```python
import functools
import math

import jax
import jax.numpy as jnp
from jax import lax
from jax.experimental import pallas as pl
from jax.experimental.pallas import tpu as pltpu
from jax.sharding import Mesh, PartitionSpec as P

EPS = 1e-06
LANES = 128
INTER = ("yh", "yl", "zl", "x")
FIRST = ("x", "yl")
SECOND = ("yh", "zl")
F32 = jnp.float32
BF16 = jnp.bfloat16
VMEM = pl.BlockSpec(memory_space=pltpu.VMEM)
PARAMS = pltpu.CompilerParams(vmem_limit_bytes=16 << 20)


def requantized(blocks):
    scales = (jnp.max(jnp.abs(blocks), axis=-1, keepdims=True) + EPS).astype(BF16).astype(F32)
    values = (blocks / scales).astype(BF16).astype(F32)
    return values * scales


def quantize_kernel(w_ref, out_ref):
    out_ref[...] = requantized(w_ref[...]).astype(BF16)


def quantize_weight(weight):
    return pl.pallas_call(
        quantize_kernel,
        out_shape=jax.ShapeDtypeStruct(weight.shape, BF16),
        in_specs=[VMEM],
        out_specs=VMEM,
        cost_estimate=pl.CostEstimate(flops=10**10, bytes_accessed=0, transcendentals=0),
        compiler_params=PARAMS,
    )(weight)


def quotient(number, by, count):
    return sum((number >= by * k).astype(jnp.int32) for k in range(1, count))


def permutation(tokens, held, wanted):
    new = lax.broadcasted_iota(jnp.int32, (tokens, tokens), 0)
    old = lax.broadcasted_iota(jnp.int32, (tokens, tokens), 1)
    sizes = dict(held)
    own = tokens // math.prod(sizes.values())
    index, rest, stride = {}, new, tokens
    for axis in wanted:
        stride //= sizes[axis]
        index[axis] = quotient(rest, stride, sizes[axis])
        rest = rest - index[axis] * stride
    source = jnp.zeros_like(new)
    for axis, size in held:
        source = source * size + index[axis]
    source = source * own + rest
    return (source == old).astype(F32).astype(BF16)


def gate_kernel(orders, pos_ref, wa_ref, wb_ref, x_ref, c_ref, part_ref, keep_ref, send_ref, w32, wmat):
    core = pos_ref[1]
    rows = wmat.shape[0]
    chunk, block = wa_ref.shape
    per_row = w32.shape[1] // rows
    lanes = w32.shape[2]
    halves = block // lanes
    for i, w_ref in enumerate((wa_ref, wb_ref)):
        for k in range(halves):
            half = w_ref[:, k * lanes : (k + 1) * lanes].astype(F32)
            w32[k, i * chunk : (i + 1) * chunk] = half
    proj = jnp.zeros((rows, x_ref.shape[0]), F32)
    for b in range(per_row):
        columns = slice(b * block, (b + 1) * block)
        w = jnp.concatenate(
            [w32[k, pl.ds(b, rows, stride=per_row), :] for k in range(halves)], axis=1
        ).astype(BF16)
        wmat[:, columns] = w
        proj += lax.dot_general(
            w, x_ref[:, columns], (((1,), (1,)), ((), ())), preferred_element_type=F32
        )
    quarter = rows // 4
    eighth = quarter // 2
    cot = c_ref[...].astype(F32)
    low = jnp.concatenate([cot[:eighth], cot[quarter : quarter + eighth]], axis=0)
    high = jnp.concatenate([cot[eighth:quarter], cot[quarter + eighth :]], axis=0)
    pre = []
    for dc in range(2):
        base = dc * 2 * quarter
        gate = proj[base : base + quarter]
        upper = proj[base + quarter : base + 2 * quarter]
        c = jnp.where(core == dc, low, high)
        sig = jax.nn.sigmoid(gate)
        pre.append(c * upper * sig * (1.0 + gate * (1.0 - sig)))
        pre.append(c * gate * sig)
    keep = jnp.concatenate(pre[:2], axis=0)
    send = jnp.concatenate(pre[2:], axis=0)
    keep_ref[...] = keep.astype(BF16)
    send_ref[...] = send.astype(BF16)
    pre = jnp.concatenate([keep, send], axis=0).astype(BF16)
    pre = lax.dot_general(
        permutation(x_ref.shape[0], *orders),
        pre,
        (((1,), (1,)), ((), ())),
        preferred_element_type=F32,
    ).astype(BF16)
    for b in range(per_row):
        columns = slice(b * block, (b + 1) * block)
        part_ref[:, columns] = jnp.dot(
            pre, wmat[:, columns], preferred_element_type=F32
        ).astype(BF16)


def gate_part(orders, pos, w_mine, w_other, x, cot):
    tokens, width = x.shape
    rows = 2 * cot.shape[0]
    block = w_mine.shape[1]
    return pl.pallas_call(
        functools.partial(gate_kernel, orders),
        out_shape=(
            jax.ShapeDtypeStruct((tokens, width), BF16),
            jax.ShapeDtypeStruct((rows // 2, tokens), BF16),
            jax.ShapeDtypeStruct((rows // 2, tokens), BF16),
        ),
        in_specs=[pl.BlockSpec(memory_space=pltpu.SMEM), VMEM, VMEM, VMEM, VMEM],
        out_specs=(VMEM, VMEM, VMEM),
        scratch_shapes=[
            pltpu.VMEM((block // LANES, 2 * w_mine.shape[0], LANES), F32),
            pltpu.VMEM((rows, width), BF16),
        ],
        compiler_params=PARAMS,
    )(pos, w_mine, w_other, x, cot)


def weight_grad_kernel(steps, pos_ref, mine_ref, got_ref, x_ref, xo_ref, *refs):
    outs, g32 = refs[: len(steps)], refs[len(steps)]
    zh = pos_ref[0]
    rows = mine_ref.shape[0]
    chunk, block = outs[0].shape
    n_z = len(steps)
    per_row = n_z * chunk // rows
    lanes = g32.shape[2]
    for b in range(per_row):
        columns = slice(b * block, (b + 1) * block)
        local = requantized(
            jnp.dot(mine_ref[...], x_ref[:, columns], preferred_element_type=F32)
        ) + requantized(jnp.dot(got_ref[...], xo_ref[:, columns], preferred_element_type=F32))
        for k in range(block // lanes):
            g32[k, pl.ds(b, rows, stride=per_row), :] = local[:, k * lanes : (k + 1) * lanes]
    for out, dz in zip(outs, steps):
        at = pl.multiple_of(lax.rem(zh + dz, n_z) * chunk, 8)
        for k in range(block // lanes):
            piece = g32[k, pl.ds(at, chunk), :]
            out[:, k * lanes : (k + 1) * lanes] = piece.astype(out.dtype)


def weight_grad_part(steps, pos, mine, got, x, x_other, chunk, block):
    return pl.pallas_call(
        functools.partial(weight_grad_kernel, steps),
        out_shape=[
            jax.ShapeDtypeStruct((chunk, block), BF16 if dz else F32) for dz in steps
        ],
        in_specs=[pl.BlockSpec(memory_space=pltpu.SMEM)] + [VMEM] * 4,
        out_specs=[VMEM] * len(steps),
        scratch_shapes=[pltpu.VMEM((block // LANES, len(steps) * chunk, LANES), F32)],
        compiler_params=PARAMS,
    )(pos, mine, got, x, x_other)


def total_kernel(scale, total_ref, *refs):
    total = total_ref[...]
    for piece in refs[:-1]:
        total = total + piece[...].astype(F32)
    refs[-1][...] = total * scale


def scaled_total(scale, total, pieces):
    return pl.pallas_call(
        functools.partial(total_kernel, scale),
        out_shape=jax.ShapeDtypeStruct(total.shape, F32),
        in_specs=[VMEM] * (1 + len(pieces)),
        out_specs=VMEM,
        cost_estimate=pl.CostEstimate(flops=10**11, bytes_accessed=0, transcendentals=0),
        compiler_params=PARAMS,
    )(total, *pieces)


def step(array, axis, by):
    n = lax.axis_size(axis)
    return lax.ppermute(array, axis, [(i, (i + by) % n) for i in range(n)])


def swapped(array):
    return lax.ppermute(array, "c", [(0, 1), (1, 0)])


def summed_pieces(pieces):
    return jnp.sum(pieces.astype(F32), axis=0).astype(BF16)


def spread(array, axes):
    return lax.all_to_all(array, axes, split_axis=0, concat_axis=0, tiled=True)


def body(activations, hidden_cot, weight):
    tok = activations.shape[1] * activations.shape[2]
    width = activations.shape[3]
    hidden = hidden_cot.shape[3]
    n_z = lax.axis_size("zh")
    x = activations.reshape(tok, width)
    cot = hidden_cot.reshape(tok, hidden).T
    pos = jnp.stack([lax.axis_index("zh"), lax.axis_index("c")]).astype(jnp.int32)
    chunk, block = weight.shape

    own = quantize_weight(weight)
    w_mine = lax.all_gather(own, "zh", axis=0, tiled=True)
    w_mine, x_late = lax.optimization_barrier((w_mine, x))
    w_other = swapped(w_mine)
    x_other = swapped(x_late)
    held = tuple((axis, lax.axis_size(axis)) for axis in INTER)
    part, keep, send = gate_part((held, FIRST + SECOND), pos, w_mine, w_other, x, cot)

    first = math.prod(lax.axis_size(axis) for axis in FIRST)
    second = math.prod(lax.axis_size(axis) for axis in SECOND)
    rows = spread(part.reshape(first, -1, width), FIRST)
    got = swapped(send)
    steps = (0, n_z // 2) + tuple(dz for dz in range(1, n_z) if dz != n_z // 2)
    total, *chunks = weight_grad_part(steps, pos, keep, got, x, x_other, chunk, block)
    rows, _ = lax.optimization_barrier((rows, chunks))
    arrived = [step(piece, "zh", dz) for piece, dz in zip(chunks, steps[1:])]
    rows = summed_pieces(rows)
    rows = spread(rows.reshape(second, -1, width), SECOND)
    input_grad = summed_pieces(rows).reshape(1, -1, activations.shape[2], width)
    scale = 1.0 / math.sqrt(tok * n_z * lax.axis_size("c"))
    weight_grad = scaled_total(scale, total, arrived)
    return (weight_grad, input_grad)


def solution(mesh):
    fine = Mesh(mesh.devices.reshape(4, 2, 3, 4, 4, 2), INTER + ("zh", "c"))
    return jax.shard_map(
        body,
        mesh=fine,
        in_specs=(
            P(("zh", "c"), None, None, None),
            P(("zh", "c"), None, None, INTER),
            P(INTER + ("zh", "c"), None),
        ),
        out_specs=(P(INTER + ("zh", "c"), None), P(("zh", "c"), INTER, None, None)),
        check_vma=False,
    )
```

```python
import functools
import math

import jax
import jax.numpy as jnp
from jax import lax
from jax.experimental import pallas as pl
from jax.experimental.pallas import tpu as pltpu
from jax.sharding import Mesh, PartitionSpec as P

EPS = 1e-06
LANES = 128
INTER = ("yh", "yl", "zl", "x")
FIRST = ("x", "yl")
SECOND = ("yh", "zl")
F32 = jnp.float32
BF16 = jnp.bfloat16
VMEM = pl.BlockSpec(memory_space=pltpu.VMEM)
SPANS = 10
PARAMS = pltpu.CompilerParams(vmem_limit_bytes=16 << 20)


def requantized(blocks):
    scales = (jnp.max(jnp.abs(blocks), axis=-1, keepdims=True) + EPS).astype(BF16).astype(F32)
    values = (blocks / scales).astype(BF16).astype(F32)
    return values * scales


def quantize_kernel(w_ref, out_ref):
    out_ref[...] = requantized(w_ref[...]).astype(BF16)


def quantize_weight(weight):
    return pl.pallas_call(
        quantize_kernel,
        out_shape=jax.ShapeDtypeStruct(weight.shape, BF16),
        in_specs=[VMEM],
        out_specs=VMEM,
        cost_estimate=pl.CostEstimate(flops=10**10, bytes_accessed=0, transcendentals=0),
        compiler_params=PARAMS,
    )(weight)


def quotient(number, by, count):
    return sum((number >= by * k).astype(jnp.int32) for k in range(1, count))


def permutation(tokens, held, wanted):
    new = lax.broadcasted_iota(jnp.int32, (tokens, tokens), 0)
    old = lax.broadcasted_iota(jnp.int32, (tokens, tokens), 1)
    sizes = dict(held)
    own = tokens // math.prod(sizes.values())
    index, rest, stride = {}, new, tokens
    for axis in wanted:
        stride //= sizes[axis]
        index[axis] = quotient(rest, stride, sizes[axis])
        rest = rest - index[axis] * stride
    source = jnp.zeros_like(new)
    for axis, size in held:
        source = source * size + index[axis]
    source = source * own + rest
    return (source == old).astype(F32).astype(BF16)


def gate_kernel(orders, pos_ref, wa_ref, wb_ref, x_ref, c_ref, part_hbm, keep_ref, send_ref, w32, wmat, part_ref, sem):
    core = pos_ref[1]
    rows = wmat.shape[0]
    span = part_ref.shape[1] // SPANS
    stores = []
    for i in range(SPANS):
        at = slice(i * span, (i + 1) * span)
        stores.append(pltpu.make_async_copy(part_ref.at[:, at], part_hbm.at[:, at], sem.at[i]))
    chunk, block = wa_ref.shape
    per_row = w32.shape[1] // rows
    lanes = w32.shape[2]
    halves = block // lanes
    for i, w_ref in enumerate((wa_ref, wb_ref)):
        for k in range(halves):
            half = w_ref[:, k * lanes : (k + 1) * lanes].astype(F32)
            w32[k, i * chunk : (i + 1) * chunk] = half
    proj = jnp.zeros((rows, x_ref.shape[0]), F32)
    for b in range(per_row):
        columns = slice(b * block, (b + 1) * block)
        w = jnp.concatenate(
            [w32[k, pl.ds(b, rows, stride=per_row), :] for k in range(halves)], axis=1
        ).astype(BF16)
        wmat[:, columns] = w
        proj += lax.dot_general(
            w, x_ref[:, columns], (((1,), (1,)), ((), ())), preferred_element_type=F32
        )
    quarter = rows // 4
    eighth = quarter // 2
    cot = c_ref[...].astype(F32)
    low = jnp.concatenate([cot[:eighth], cot[quarter : quarter + eighth]], axis=0)
    high = jnp.concatenate([cot[eighth:quarter], cot[quarter + eighth :]], axis=0)
    pre = []
    for dc in range(2):
        base = dc * 2 * quarter
        gate = proj[base : base + quarter]
        upper = proj[base + quarter : base + 2 * quarter]
        c = jnp.where(core == dc, low, high)
        sig = jax.nn.sigmoid(gate)
        pre.append(c * upper * sig * (1.0 + gate * (1.0 - sig)))
        pre.append(c * gate * sig)
    keep = jnp.concatenate(pre[:2], axis=0)
    send = jnp.concatenate(pre[2:], axis=0)
    keep_ref[...] = keep.astype(BF16)
    send_ref[...] = send.astype(BF16)
    pre = jnp.concatenate([keep, send], axis=0).astype(BF16)
    pre = lax.dot_general(
        permutation(x_ref.shape[0], *orders),
        pre,
        (((1,), (1,)), ((), ())),
        preferred_element_type=F32,
    ).astype(BF16)
    for b in range(per_row):
        columns = slice(b * block, (b + 1) * block)
        part_ref[:, columns] = jnp.dot(
            pre, wmat[:, columns], preferred_element_type=F32
        ).astype(BF16)
        if (b + 1) * block % span == 0:
            stores[b * block // span].start()
    for store in stores:
        store.wait()


def gate_part(orders, pos, w_mine, w_other, x, cot):
    tokens, width = x.shape
    rows = 2 * cot.shape[0]
    block = w_mine.shape[1]
    return pl.pallas_call(
        functools.partial(gate_kernel, orders),
        out_shape=(
            pltpu.HBM((tokens, width), BF16),
            jax.ShapeDtypeStruct((rows // 2, tokens), BF16),
            jax.ShapeDtypeStruct((rows // 2, tokens), BF16),
        ),
        in_specs=[pl.BlockSpec(memory_space=pltpu.SMEM), VMEM, VMEM, VMEM, VMEM],
        out_specs=(pl.BlockSpec(memory_space=pltpu.HBM), VMEM, VMEM),
        scratch_shapes=[
            pltpu.VMEM((block // LANES, 2 * w_mine.shape[0], LANES), F32),
            pltpu.VMEM((rows, width), BF16),
            pltpu.VMEM((tokens, width), BF16),
            pltpu.SemaphoreType.DMA((SPANS,)),
        ],
        compiler_params=pltpu.CompilerParams(vmem_limit_bytes=16 << 20),
    )(pos, w_mine, w_other, x, cot)


def weight_grad_kernel(steps, pos_ref, mine_ref, got_ref, x_ref, xo_ref, *refs):
    outs, g32 = refs[: len(steps)], refs[len(steps)]
    zh = pos_ref[0]
    rows = mine_ref.shape[0]
    chunk, block = outs[0].shape
    n_z = len(steps)
    per_row = n_z * chunk // rows
    lanes = g32.shape[2]
    for b in range(per_row):
        columns = slice(b * block, (b + 1) * block)
        local = requantized(
            jnp.dot(mine_ref[...], x_ref[:, columns], preferred_element_type=F32)
        ) + requantized(jnp.dot(got_ref[...], xo_ref[:, columns], preferred_element_type=F32))
        for k in range(block // lanes):
            g32[k, pl.ds(b, rows, stride=per_row), :] = local[:, k * lanes : (k + 1) * lanes]
    for out, dz in zip(outs, steps):
        at = pl.multiple_of(lax.rem(zh + dz, n_z) * chunk, 8)
        for k in range(block // lanes):
            piece = g32[k, pl.ds(at, chunk), :]
            out[:, k * lanes : (k + 1) * lanes] = piece.astype(out.dtype)


def weight_grad_part(steps, pos, mine, got, x, x_other, chunk, block):
    return pl.pallas_call(
        functools.partial(weight_grad_kernel, steps),
        out_shape=[
            jax.ShapeDtypeStruct((chunk, block), BF16 if dz else F32) for dz in steps
        ],
        in_specs=[pl.BlockSpec(memory_space=pltpu.SMEM)] + [VMEM] * 4,
        out_specs=[VMEM] * len(steps),
        scratch_shapes=[pltpu.VMEM((block // LANES, len(steps) * chunk, LANES), F32)],
        compiler_params=PARAMS,
    )(pos, mine, got, x, x_other)


def total_kernel(scale, total_ref, *refs):
    total = total_ref[...]
    for piece in refs[:-1]:
        total = total + piece[...].astype(F32)
    refs[-1][...] = total * scale


def scaled_total(scale, total, pieces):
    return pl.pallas_call(
        functools.partial(total_kernel, scale),
        out_shape=jax.ShapeDtypeStruct(total.shape, F32),
        in_specs=[VMEM] * (1 + len(pieces)),
        out_specs=VMEM,
        cost_estimate=pl.CostEstimate(flops=10**11, bytes_accessed=0, transcendentals=0),
        compiler_params=PARAMS,
    )(total, *pieces)


def step(array, axis, by):
    n = lax.axis_size(axis)
    return lax.ppermute(array, axis, [(i, (i + by) % n) for i in range(n)])


def swapped(array):
    return lax.ppermute(array, "c", [(0, 1), (1, 0)])


def summed_pieces(pieces):
    return jnp.sum(pieces.astype(F32), axis=0).astype(BF16)


def spread(array, axes):
    return lax.all_to_all(array, axes, split_axis=0, concat_axis=0, tiled=True)


def body(activations, hidden_cot, weight):
    tok = activations.shape[1] * activations.shape[2]
    width = activations.shape[3]
    hidden = hidden_cot.shape[3]
    n_z = lax.axis_size("zh")
    x = activations.reshape(tok, width)
    cot = hidden_cot.reshape(tok, hidden).T
    pos = jnp.stack([lax.axis_index("zh"), lax.axis_index("c")]).astype(jnp.int32)
    chunk, block = weight.shape

    own = quantize_weight(weight)
    w_mine = lax.all_gather(own, "zh", axis=0, tiled=True)
    w_mine, x_late = lax.optimization_barrier((w_mine, x))
    w_other = swapped(w_mine)
    x_other = swapped(x_late)
    held = tuple((axis, lax.axis_size(axis)) for axis in INTER)
    part, keep, send = gate_part((held, FIRST + SECOND), pos, w_mine, w_other, x, cot)

    first = math.prod(lax.axis_size(axis) for axis in FIRST)
    second = math.prod(lax.axis_size(axis) for axis in SECOND)
    rows = spread(part.reshape(first, -1, width), FIRST)
    got = swapped(send)
    steps = (0, n_z // 2) + tuple(dz for dz in range(1, n_z) if dz != n_z // 2)
    total, *chunks = weight_grad_part(steps, pos, keep, got, x, x_other, chunk, block)
    rows, _ = lax.optimization_barrier((rows, chunks))
    arrived = [step(piece, "zh", dz) for piece, dz in zip(chunks, steps[1:])]
    rows = summed_pieces(rows)
    rows = spread(rows.reshape(second, -1, width), SECOND)
    input_grad = summed_pieces(rows).reshape(1, -1, activations.shape[2], width)
    scale = 1.0 / math.sqrt(tok * n_z * lax.axis_size("c"))
    weight_grad = scaled_total(scale, total, arrived)
    return (weight_grad, input_grad)


def solution(mesh):
    fine = Mesh(mesh.devices.reshape(4, 2, 3, 4, 4, 2), INTER + ("zh", "c"))
    return jax.shard_map(
        body,
        mesh=fine,
        in_specs=(
            P(("zh", "c"), None, None, None),
            P(("zh", "c"), None, None, INTER),
            P(INTER + ("zh", "c"), None),
        ),
        out_specs=(P(INTER + ("zh", "c"), None), P(("zh", "c"), INTER, None, None)),
        check_vma=False,
    )
```

```python
import functools
import math

import jax
import jax.numpy as jnp
from jax import lax
from jax.experimental import pallas as pl
from jax.experimental.pallas import tpu as pltpu
from jax.sharding import Mesh, PartitionSpec as P

EPS = 1e-06
LANES = 128
INTER = ("yh", "yl", "zl", "x")
FIRST = ("x", "yl")
SECOND = ("zl", "yh")
F32 = jnp.float32
BF16 = jnp.bfloat16
VMEM = pl.BlockSpec(memory_space=pltpu.VMEM)
SPANS = 10
PARAMS = pltpu.CompilerParams(vmem_limit_bytes=16 << 20)


def requantized(blocks):
    scales = (jnp.max(jnp.abs(blocks), axis=-1, keepdims=True) + EPS).astype(BF16).astype(F32)
    values = (blocks / scales).astype(BF16).astype(F32)
    return values * scales


def quantize_kernel(w_ref, out_ref):
    out_ref[...] = requantized(w_ref[...]).astype(BF16)


def quantize_weight(weight):
    return pl.pallas_call(
        quantize_kernel,
        out_shape=jax.ShapeDtypeStruct(weight.shape, BF16),
        in_specs=[VMEM],
        out_specs=VMEM,
        cost_estimate=pl.CostEstimate(flops=10**10, bytes_accessed=0, transcendentals=0),
        compiler_params=PARAMS,
    )(weight)


def quotient(number, by, count):
    return sum((number >= by * k).astype(jnp.int32) for k in range(1, count))


def permutation(tokens, held, wanted):
    new = lax.broadcasted_iota(jnp.int32, (tokens, tokens), 0)
    old = lax.broadcasted_iota(jnp.int32, (tokens, tokens), 1)
    sizes = dict(held)
    own = tokens // math.prod(sizes.values())
    index, rest, stride = {}, new, tokens
    for axis in wanted:
        stride //= sizes[axis]
        index[axis] = quotient(rest, stride, sizes[axis])
        rest = rest - index[axis] * stride
    source = jnp.zeros_like(new)
    for axis, size in held:
        source = source * size + index[axis]
    source = source * own + rest
    return (source == old).astype(F32).astype(BF16)


def gate_kernel(orders, pos_ref, wa_ref, wb_ref, x_ref, c_ref, part_hbm, keep_ref, send_ref, w32, wmat, part_ref, sem):
    core = pos_ref[1]
    rows = wmat.shape[0]
    span = part_ref.shape[1] // SPANS
    stores = []
    for i in range(SPANS):
        at = slice(i * span, (i + 1) * span)
        stores.append(pltpu.make_async_copy(part_ref.at[:, at], part_hbm.at[:, at], sem.at[i]))
    chunk, block = wa_ref.shape
    per_row = w32.shape[1] // rows
    lanes = w32.shape[2]
    halves = block // lanes
    for i, w_ref in enumerate((wa_ref, wb_ref)):
        for k in range(halves):
            half = w_ref[:, k * lanes : (k + 1) * lanes].astype(F32)
            w32[k, i * chunk : (i + 1) * chunk] = half
    proj = jnp.zeros((rows, x_ref.shape[0]), F32)
    for b in range(per_row):
        columns = slice(b * block, (b + 1) * block)
        w = jnp.concatenate(
            [w32[k, pl.ds(b, rows, stride=per_row), :] for k in range(halves)], axis=1
        ).astype(BF16)
        wmat[:, columns] = w
        proj += lax.dot_general(
            w, x_ref[:, columns], (((1,), (1,)), ((), ())), preferred_element_type=F32
        )
    quarter = rows // 4
    eighth = quarter // 2
    cot = c_ref[...].astype(F32)
    low = jnp.concatenate([cot[:eighth], cot[quarter : quarter + eighth]], axis=0)
    high = jnp.concatenate([cot[eighth:quarter], cot[quarter + eighth :]], axis=0)
    pre = []
    for dc in range(2):
        base = dc * 2 * quarter
        gate = proj[base : base + quarter]
        upper = proj[base + quarter : base + 2 * quarter]
        c = jnp.where(core == dc, low, high)
        sig = jax.nn.sigmoid(gate)
        pre.append(c * upper * sig * (1.0 + gate * (1.0 - sig)))
        pre.append(c * gate * sig)
    keep = jnp.concatenate(pre[:2], axis=0)
    send = jnp.concatenate(pre[2:], axis=0)
    keep_ref[...] = keep.astype(BF16)
    send_ref[...] = send.astype(BF16)
    pre = jnp.concatenate([keep, send], axis=0).astype(BF16)
    pre = lax.dot_general(
        permutation(x_ref.shape[0], *orders),
        pre,
        (((1,), (1,)), ((), ())),
        preferred_element_type=F32,
    ).astype(BF16)
    for b in range(per_row):
        columns = slice(b * block, (b + 1) * block)
        part_ref[:, columns] = jnp.dot(
            pre, wmat[:, columns], preferred_element_type=F32
        ).astype(BF16)
        if (b + 1) * block % span == 0:
            stores[b * block // span].start()
    for store in stores:
        store.wait()


def gate_part(orders, pos, w_mine, w_other, x, cot):
    tokens, width = x.shape
    rows = 2 * cot.shape[0]
    block = w_mine.shape[1]
    return pl.pallas_call(
        functools.partial(gate_kernel, orders),
        out_shape=(
            pltpu.HBM((tokens, width), BF16),
            jax.ShapeDtypeStruct((rows // 2, tokens), BF16),
            jax.ShapeDtypeStruct((rows // 2, tokens), BF16),
        ),
        in_specs=[pl.BlockSpec(memory_space=pltpu.SMEM), VMEM, VMEM, VMEM, VMEM],
        out_specs=(pl.BlockSpec(memory_space=pltpu.HBM), VMEM, VMEM),
        scratch_shapes=[
            pltpu.VMEM((block // LANES, 2 * w_mine.shape[0], LANES), F32),
            pltpu.VMEM((rows, width), BF16),
            pltpu.VMEM((tokens, width), BF16),
            pltpu.SemaphoreType.DMA((SPANS,)),
        ],
        compiler_params=pltpu.CompilerParams(vmem_limit_bytes=16 << 20),
    )(pos, w_mine, w_other, x, cot)


def weight_grad_kernel(steps, pos_ref, mine_ref, got_ref, x_ref, xo_ref, *refs):
    outs, g32 = refs[: len(steps)], refs[len(steps)]
    zh = pos_ref[0]
    rows = mine_ref.shape[0]
    chunk, block = outs[0].shape
    n_z = len(steps)
    per_row = n_z * chunk // rows
    lanes = g32.shape[2]
    for b in range(per_row):
        columns = slice(b * block, (b + 1) * block)
        local = requantized(
            jnp.dot(mine_ref[...], x_ref[:, columns], preferred_element_type=F32)
        ) + requantized(jnp.dot(got_ref[...], xo_ref[:, columns], preferred_element_type=F32))
        for k in range(block // lanes):
            g32[k, pl.ds(b, rows, stride=per_row), :] = local[:, k * lanes : (k + 1) * lanes]
    for out, dz in zip(outs, steps):
        at = pl.multiple_of(lax.rem(zh + dz, n_z) * chunk, 8)
        for k in range(block // lanes):
            piece = g32[k, pl.ds(at, chunk), :]
            out[:, k * lanes : (k + 1) * lanes] = piece.astype(out.dtype)


def weight_grad_part(steps, pos, mine, got, x, x_other, chunk, block):
    return pl.pallas_call(
        functools.partial(weight_grad_kernel, steps),
        out_shape=[
            jax.ShapeDtypeStruct((chunk, block), BF16 if dz else F32) for dz in steps
        ],
        in_specs=[pl.BlockSpec(memory_space=pltpu.SMEM)] + [VMEM] * 4,
        out_specs=[VMEM] * len(steps),
        scratch_shapes=[pltpu.VMEM((block // LANES, len(steps) * chunk, LANES), F32)],
        compiler_params=PARAMS,
    )(pos, mine, got, x, x_other)


def total_kernel(scale, total_ref, *refs):
    total = total_ref[...]
    for piece in refs[:-1]:
        total = total + piece[...].astype(F32)
    refs[-1][...] = total * scale


def scaled_total(scale, total, pieces):
    return pl.pallas_call(
        functools.partial(total_kernel, scale),
        out_shape=jax.ShapeDtypeStruct(total.shape, F32),
        in_specs=[VMEM] * (1 + len(pieces)),
        out_specs=VMEM,
        cost_estimate=pl.CostEstimate(flops=10**11, bytes_accessed=0, transcendentals=0),
        compiler_params=PARAMS,
    )(total, *pieces)


def step(array, axis, by):
    n = lax.axis_size(axis)
    return lax.ppermute(array, axis, [(i, (i + by) % n) for i in range(n)])


def swapped(array):
    return lax.ppermute(array, "c", [(0, 1), (1, 0)])


def summed_pieces(pieces):
    return jnp.sum(pieces.astype(F32), axis=0).astype(BF16)


def spread(array, axes):
    return lax.all_to_all(array, axes, split_axis=0, concat_axis=0, tiled=True)


def body(activations, hidden_cot, weight):
    tok = activations.shape[1] * activations.shape[2]
    width = activations.shape[3]
    hidden = hidden_cot.shape[3]
    n_z = lax.axis_size("zh")
    x = activations.reshape(tok, width)
    cot = hidden_cot.reshape(tok, hidden).T
    pos = jnp.stack([lax.axis_index("zh"), lax.axis_index("c")]).astype(jnp.int32)
    chunk, block = weight.shape

    own = quantize_weight(weight)
    w_mine = lax.all_gather(own, "zh", axis=0, tiled=True)
    w_mine, x_late = lax.optimization_barrier((w_mine, x))
    w_other = swapped(w_mine)
    x_other = swapped(x_late)
    held = tuple((axis, lax.axis_size(axis)) for axis in INTER)
    part, keep, send = gate_part((held, FIRST + SECOND), pos, w_mine, w_other, x, cot)

    first = math.prod(lax.axis_size(axis) for axis in FIRST)
    second = math.prod(lax.axis_size(axis) for axis in SECOND)
    rows = spread(part.reshape(first, -1, width), FIRST)
    got = swapped(send)
    steps = (0, n_z // 2) + tuple(dz for dz in range(1, n_z) if dz != n_z // 2)
    total, *chunks = weight_grad_part(steps, pos, keep, got, x, x_other, chunk, block)
    rows, _ = lax.optimization_barrier((rows, chunks))
    arrived = [step(piece, "zh", dz) for piece, dz in zip(chunks, steps[1:])]
    rows = summed_pieces(rows)
    rows = spread(rows.reshape(second, -1, width), SECOND)
    input_grad = summed_pieces(rows).reshape(1, -1, activations.shape[2], width)
    scale = 1.0 / math.sqrt(tok * n_z * lax.axis_size("c"))
    weight_grad = scaled_total(scale, total, arrived)
    return (weight_grad, input_grad)


def solution(mesh):
    fine = Mesh(mesh.devices.reshape(4, 2, 3, 4, 4, 2), INTER + ("zh", "c"))
    return jax.shard_map(
        body,
        mesh=fine,
        in_specs=(
            P(("zh", "c"), None, None, None),
            P(("zh", "c"), None, None, INTER),
            P(INTER + ("zh", "c"), None),
        ),
        out_specs=(P(INTER + ("zh", "c"), None), P(("zh", "c"), INTER, None, None)),
        check_vma=False,
    )
```

```python
import functools
import math

import jax
import jax.numpy as jnp
from jax import lax
from jax.experimental import pallas as pl
from jax.experimental.pallas import tpu as pltpu
from jax.sharding import Mesh, PartitionSpec as P

EPS = 1e-06
LANES = 128
INTER = ("yh", "yl", "zl", "x")
FIRST = ("x", "yl")
SECOND = ("zl", "yh")
F32 = jnp.float32
BF16 = jnp.bfloat16
VMEM = pl.BlockSpec(memory_space=pltpu.VMEM)
SPANS = 10
PARAMS = pltpu.CompilerParams(vmem_limit_bytes=16 << 20)


def requantized(blocks):
    scales = (jnp.max(jnp.abs(blocks), axis=-1, keepdims=True) + EPS).astype(BF16).astype(F32)
    values = (blocks / scales).astype(BF16).astype(F32)
    return values * scales


def quantize_kernel(w_ref, out_ref):
    out_ref[...] = requantized(w_ref[...]).astype(BF16)


def quantize_weight(weight):
    return pl.pallas_call(
        quantize_kernel,
        out_shape=jax.ShapeDtypeStruct(weight.shape, BF16),
        in_specs=[VMEM],
        out_specs=VMEM,
        cost_estimate=pl.CostEstimate(flops=10**10, bytes_accessed=0, transcendentals=0),
        compiler_params=PARAMS,
    )(weight)


def quotient(number, by, count):
    return sum((number >= by * k).astype(jnp.int32) for k in range(1, count))


def permutation(tokens, held, wanted):
    new = lax.broadcasted_iota(jnp.int32, (tokens, tokens), 0)
    old = lax.broadcasted_iota(jnp.int32, (tokens, tokens), 1)
    sizes = dict(held)
    own = tokens // math.prod(sizes.values())
    index, rest, stride = {}, new, tokens
    for axis in wanted:
        stride //= sizes[axis]
        index[axis] = quotient(rest, stride, sizes[axis])
        rest = rest - index[axis] * stride
    source = jnp.zeros_like(new)
    for axis, size in held:
        source = source * size + index[axis]
    source = source * own + rest
    return (source == old).astype(F32).astype(BF16)


def gate_kernel(orders, pos_ref, wa_ref, wb_ref, x_ref, c_ref, part_hbm, keep_ref, send_ref, w32, wmat, part_ref, sem):
    core = pos_ref[1]
    rows = wmat.shape[0]
    span = part_ref.shape[1] // SPANS
    stores = []
    for i in range(SPANS):
        at = slice(i * span, (i + 1) * span)
        stores.append(pltpu.make_async_copy(part_ref.at[:, at], part_hbm.at[:, at], sem.at[i]))
    chunk, block = wa_ref.shape
    per_row = w32.shape[1] // rows
    lanes = w32.shape[2]
    halves = block // lanes
    for i, w_ref in enumerate((wa_ref, wb_ref)):
        for k in range(halves):
            half = w_ref[:, k * lanes : (k + 1) * lanes].astype(F32)
            w32[k, i * chunk : (i + 1) * chunk] = half
    proj = jnp.zeros((rows, x_ref.shape[0]), F32)
    for b in range(per_row):
        columns = slice(b * block, (b + 1) * block)
        w = jnp.concatenate(
            [w32[k, pl.ds(b, rows, stride=per_row), :] for k in range(halves)], axis=1
        ).astype(BF16)
        wmat[:, columns] = w
        proj += lax.dot_general(
            w, x_ref[:, columns], (((1,), (1,)), ((), ())), preferred_element_type=F32
        )
    quarter = rows // 4
    eighth = quarter // 2
    cot = c_ref[...].astype(F32)
    low = jnp.concatenate([cot[:eighth], cot[quarter : quarter + eighth]], axis=0)
    high = jnp.concatenate([cot[eighth:quarter], cot[quarter + eighth :]], axis=0)
    pre = []
    for dc in range(2):
        base = dc * 2 * quarter
        gate = proj[base : base + quarter]
        upper = proj[base + quarter : base + 2 * quarter]
        c = jnp.where(core == dc, low, high)
        sig = jax.nn.sigmoid(gate)
        pre.append(c * upper * sig * (1.0 + gate * (1.0 - sig)))
        pre.append(c * gate * sig)
    keep = jnp.concatenate(pre[:2], axis=0)
    send = jnp.concatenate(pre[2:], axis=0)
    keep_ref[...] = keep.astype(BF16)
    send_ref[...] = send.astype(BF16)
    pre = jnp.concatenate([keep, send], axis=0).astype(BF16)
    pre = lax.dot_general(
        permutation(x_ref.shape[0], *orders),
        pre,
        (((1,), (1,)), ((), ())),
        preferred_element_type=F32,
    ).astype(BF16)
    for b in range(per_row):
        columns = slice(b * block, (b + 1) * block)
        part_ref[:, columns] = jnp.dot(
            pre, wmat[:, columns], preferred_element_type=F32
        ).astype(BF16)
        if (b + 1) * block % span == 0:
            stores[b * block // span].start()
    for store in stores:
        store.wait()


def gate_part(orders, pos, w_mine, w_other, x, cot):
    tokens, width = x.shape
    rows = 2 * cot.shape[0]
    block = w_mine.shape[1]
    return pl.pallas_call(
        functools.partial(gate_kernel, orders),
        out_shape=(
            pltpu.HBM((tokens, width), BF16),
            jax.ShapeDtypeStruct((rows // 2, tokens), BF16),
            jax.ShapeDtypeStruct((rows // 2, tokens), BF16),
        ),
        in_specs=[pl.BlockSpec(memory_space=pltpu.SMEM), VMEM, VMEM, VMEM, VMEM],
        out_specs=(pl.BlockSpec(memory_space=pltpu.HBM), VMEM, VMEM),
        scratch_shapes=[
            pltpu.VMEM((block // LANES, 2 * w_mine.shape[0], LANES), F32),
            pltpu.VMEM((rows, width), BF16),
            pltpu.VMEM((tokens, width), BF16),
            pltpu.SemaphoreType.DMA((SPANS,)),
        ],
        compiler_params=pltpu.CompilerParams(vmem_limit_bytes=16 << 20),
    )(pos, w_mine, w_other, x, cot)


def weight_grad_kernel(steps, pos_ref, mine_ref, got_ref, x_ref, xo_ref, *refs):
    outs, g32 = refs[: len(steps)], refs[len(steps)]
    zh = pos_ref[0]
    rows = mine_ref.shape[0]
    chunk, block = outs[0].shape
    n_z = len(steps)
    per_row = n_z * chunk // rows
    lanes = g32.shape[2]
    for b in range(per_row):
        columns = slice(b * block, (b + 1) * block)
        local = requantized(
            jnp.dot(mine_ref[...], x_ref[:, columns], preferred_element_type=F32)
        ) + requantized(jnp.dot(got_ref[...], xo_ref[:, columns], preferred_element_type=F32))
        for k in range(block // lanes):
            g32[k, pl.ds(b, rows, stride=per_row), :] = local[:, k * lanes : (k + 1) * lanes]
    for out, dz in zip(outs, steps):
        at = pl.multiple_of(lax.rem(zh + dz, n_z) * chunk, 8)
        for k in range(block // lanes):
            piece = g32[k, pl.ds(at, chunk), :]
            out[:, k * lanes : (k + 1) * lanes] = piece.astype(out.dtype)


def weight_grad_part(steps, pos, mine, got, x, x_other, chunk, block):
    return pl.pallas_call(
        functools.partial(weight_grad_kernel, steps),
        out_shape=[
            jax.ShapeDtypeStruct((chunk, block), BF16 if dz else F32) for dz in steps
        ],
        in_specs=[pl.BlockSpec(memory_space=pltpu.SMEM)] + [VMEM] * 4,
        out_specs=[VMEM] * len(steps),
        scratch_shapes=[pltpu.VMEM((block // LANES, len(steps) * chunk, LANES), F32)],
        compiler_params=PARAMS,
    )(pos, mine, got, x, x_other)


def total_kernel(scale, total_ref, *refs):
    total = total_ref[...]
    for piece in refs[:-1]:
        total = total + piece[...].astype(F32)
    refs[-1][...] = total * scale


def scaled_total(scale, total, pieces):
    return pl.pallas_call(
        functools.partial(total_kernel, scale),
        out_shape=jax.ShapeDtypeStruct(total.shape, F32),
        in_specs=[VMEM] * (1 + len(pieces)),
        out_specs=VMEM,
        cost_estimate=pl.CostEstimate(flops=10**11, bytes_accessed=0, transcendentals=0),
        compiler_params=PARAMS,
    )(total, *pieces)


def step(array, axis, by):
    n = lax.axis_size(axis)
    return lax.ppermute(array, axis, [(i, (i + by) % n) for i in range(n)])


def swapped(array):
    return lax.ppermute(array, "c", [(0, 1), (1, 0)])


def sum_kernel(pieces_ref, out_ref):
    total = pieces_ref[0].astype(F32)
    for i in range(1, pieces_ref.shape[0]):
        total = total + pieces_ref[i].astype(F32)
    out_ref[...] = total.astype(BF16).reshape(out_ref.shape)


def summed_pieces(pieces, shape):
    return pl.pallas_call(
        sum_kernel,
        out_shape=pltpu.HBM(shape, BF16),
        in_specs=[VMEM],
        out_specs=VMEM,
        compiler_params=PARAMS,
    )(pieces)


def spread(array, axes):
    return lax.all_to_all(array, axes, split_axis=0, concat_axis=0, tiled=True)


def body(activations, hidden_cot, weight):
    tok = activations.shape[1] * activations.shape[2]
    width = activations.shape[3]
    hidden = hidden_cot.shape[3]
    n_z = lax.axis_size("zh")
    x = activations.reshape(tok, width)
    cot = hidden_cot.reshape(tok, hidden).T
    pos = jnp.stack([lax.axis_index("zh"), lax.axis_index("c")]).astype(jnp.int32)
    chunk, block = weight.shape

    own = quantize_weight(weight)
    w_mine = lax.all_gather(own, "zh", axis=0, tiled=True)
    w_mine, x_late = lax.optimization_barrier((w_mine, x))
    w_other = swapped(w_mine)
    x_other = swapped(x_late)
    held = tuple((axis, lax.axis_size(axis)) for axis in INTER)
    part, keep, send = gate_part((held, FIRST + SECOND), pos, w_mine, w_other, x, cot)

    first = math.prod(lax.axis_size(axis) for axis in FIRST)
    second = math.prod(lax.axis_size(axis) for axis in SECOND)
    rows = spread(part.reshape(first, -1, width), FIRST)
    got = swapped(send)
    steps = (0, n_z // 2) + tuple(dz for dz in range(1, n_z) if dz != n_z // 2)
    total, *chunks = weight_grad_part(steps, pos, keep, got, x, x_other, chunk, block)
    rows, _ = lax.optimization_barrier((rows, chunks))
    arrived = [step(piece, "zh", dz) for piece, dz in zip(chunks, steps[1:])]
    left = tok // (first * second)
    rows = summed_pieces(rows, (second, left, width))
    rows = spread(rows, SECOND)
    rows = jnp.sum(rows.astype(F32), axis=0).astype(BF16)
    input_grad = rows.reshape(1, left, activations.shape[2], width)
    scale = 1.0 / math.sqrt(tok * n_z * lax.axis_size("c"))
    weight_grad = scaled_total(scale, total, arrived)
    return (weight_grad, input_grad)


def solution(mesh):
    fine = Mesh(mesh.devices.reshape(4, 2, 3, 4, 4, 2), INTER + ("zh", "c"))
    return jax.shard_map(
        body,
        mesh=fine,
        in_specs=(
            P(("zh", "c"), None, None, None),
            P(("zh", "c"), None, None, INTER),
            P(INTER + ("zh", "c"), None),
        ),
        out_specs=(P(INTER + ("zh", "c"), None), P(("zh", "c"), INTER, None, None)),
        check_vma=False,
    )
```
